32 devices in a mesh: rows: 8 (over z, y), chan: 4 (over x, core).
Axes of the slice: x: 2, y: 2, z: 4, core: 2. Of those that a mesh axis runs over, the one named last changes fastest.
Arguments:
- images: bfloat16 [64, 28, 28, 2016], P(('rows', 'chan')), may hold values from -6 to 6
- counts: int32 [32], replicated, may hold values from 1 to 2, as said below
- out_grad: bfloat16 [64, 14, 14, 2016], P(('rows', 'chan')), may hold values from -6 to 6
- pointwise_w: float32 [5, 2016, 2016], P(None, 'rows', 'chan'), may hold values from -0.125 to 0.125
- grouped_w: float32 [2, 9, 56, 2016], P(None, None, None, 'rows'), may hold values from -0.25 to 0.25
- squeeze_w: float32 [2, 2016, 504], P(None, 'rows'), may hold values from -0.125 to 0.125
- excite_w: float32 [2, 504, 2016], P(None, None, 'rows'), may hold values from -0.25 to 0.25
- norm_params: float32 [2, 7, 2016], P(None, None, 'rows'), may hold values from 0.25 to 1.25
- pointwise_m: float32 [5, 2016, 2016], P(None, 'rows', 'chan'), may hold values from -0.0625 to 0.0625
- grouped_m: float32 [2, 9, 56, 2016], P(None, None, None, 'rows'), may hold values from -0.125 to 0.125
- squeeze_m: float32 [2, 2016, 504], P(None, 'rows'), may hold values from -0.0625 to 0.0625
- excite_m: float32 [2, 504, 2016], P(None, None, 'rows'), may hold values from -0.125 to 0.125
- norm_m: float32 [2, 7, 2016], P(None, None, 'rows'), may hold values from -1.5 to 1.5
Outputs:
- activations: bfloat16 [64, 14, 14, 2016], P(('rows', 'chan'))
- input_grad: bfloat16 [64, 28, 28, 2016], P(('rows', 'chan'))
- layer_norms: float32 [2, 11], replicated
- grad_pointwise: float32 [5, 2016, 2016], P(None, 'rows', 'chan')
- grad_grouped: float32 [2, 9, 56, 2016], P(None, None, None, 'rows')
- grad_squeeze: float32 [2, 2016, 504], P(None, 'rows')
- grad_excite: float32 [2, 504, 2016], P(None, None, 'rows')
- grad_norm: float32 [2, 7, 2016], P(None, None, 'rows')
- moment_pointwise: float32 [5, 2016, 2016], P(None, 'rows', 'chan')
- moment_grouped: float32 [2, 9, 56, 2016], P(None, None, None, 'rows')
- moment_squeeze: float32 [2, 2016, 504], P(None, 'rows')
- moment_excite: float32 [2, 504, 2016], P(None, None, 'rows')
- moment_norm: float32 [2, 7, 2016], P(None, None, 'rows')
- new_pointwise: float32 [5, 2016, 2016], P(None, 'rows', 'chan')
- new_grouped: float32 [2, 9, 56, 2016], P(None, None, None, 'rows')
- new_squeeze: float32 [2, 2016, 504], P(None, 'rows')
- new_excite: float32 [2, 504, 2016], P(None, None, 'rows')
- new_norm: float32 [2, 7, 2016], P(None, None, 'rows')
The draws below stay inside these ranges and needn't reach their ends.
Inputs may be any that keep to these rules, and one draw needn't show every extreme that they name: `counts`: some device holds 2 live images; live images are the first slots of a device.
All inputs are finite; a program needn't handle non-finite values.
Results may differ from the reference program's by a relative error of at most 0.025.
Values may be sent and summed in bfloat16 or wider, within the bound.
No kernel may reach another device: no remote copies, remote signals or barrier semaphores. Data moves between devices by JAX's collectives and lax.ppermute only.
A program may use at most 704 MiB of HBM per device.

```python
import jax
import jax.numpy as jnp
from jax import lax

C = 2016
GROUPS = 36
GW = 56
SE_DIM = 504
HO = 14
IMG_CAP = 2
HI = 28
SHARDS = 32
IMAGES = 64


def draw_counts(key, part):
    key = jax.random.fold_in(key, 11)
    first_key, second_key = jax.random.split(key)
    drawn = jax.random.randint(first_key, (SHARDS,), 1, IMG_CAP + 1)
    fullest = jax.random.randint(second_key, (), 0, SHARDS)
    return drawn.at[fullest].set(IMG_CAP).astype(jnp.int32)


def level_of(key, extent, cuts, smallest, high):
    def one(dim, blocks):
        heights = jax.random.uniform(jax.random.fold_in(jax.random.fold_in(key, 6), dim), (blocks,), jnp.float32, smallest / len(cuts), high / len(cuts))
        return jnp.repeat(jnp.exp(heights), extent[dim] // blocks).reshape((-1,) + (1,) * (len(extent) - dim - 1))

    factor_of = one(*cuts[0])
    for cut in cuts[1:]:
        factor_of = factor_of * one(*cut)
    return factor_of


def centred(rng, extent, deviation, reach, cuts=(), kind=jnp.bfloat16):
    loudness = level_of(rng, extent, cuts, -0.22, 0.18) if cuts else 1.0
    values = jax.random.normal(rng, extent, jnp.float32) * deviation * loudness
    return jnp.minimum(jnp.maximum(values, -reach), reach).astype(kind)


def setup_inputs(seed: int = 0) -> dict:
    arg_keys = jax.random.split(jax.random.key(seed), 14)
    return {
        "images": centred(arg_keys[0], (IMAGES, HI, HI, C), 1.0, 6.0, ((0, 32),)),
        "counts": draw_counts(jax.random.fold_in(arg_keys[13], 71), 0),
        "out_grad": centred(arg_keys[2], (IMAGES, HO, HO, C), 1.0, 6.0, ((0, 32),)),
        "pointwise_w": centred(arg_keys[3], (5, C, C), C ** -0.5, 0.125, ((1, 8), (2, 4)), jnp.float32),
        "grouped_w": centred(arg_keys[4], (2, 9, GW, C), (9 * GW) ** -0.5, 0.25, ((3, 8),), jnp.float32),
        "squeeze_w": centred(arg_keys[5], (2, C, SE_DIM), C ** -0.5, 0.125, ((1, 8),), jnp.float32),
        "excite_w": centred(arg_keys[6], (2, SE_DIM, C), SE_DIM ** -0.5, 0.25, ((2, 8),), jnp.float32),
        "norm_params": jnp.clip(0.25 + 1.0 * jax.random.uniform(arg_keys[7], (2, 7, C), jnp.float32) ** level_of(arg_keys[7], (2, 7, C), ((2, 8),), -0.2, 0.2), 0.25, 1.25),
        "pointwise_m": centred(arg_keys[8], (5, C, C), 0.004, 0.0625, ((1, 8), (2, 4)), jnp.float32),
        "grouped_m": centred(arg_keys[9], (2, 9, GW, C), 0.008, 0.125, ((3, 8),), jnp.float32),
        "squeeze_m": centred(arg_keys[10], (2, C, SE_DIM), 0.004, 0.0625, ((1, 8),), jnp.float32),
        "excite_m": centred(arg_keys[11], (2, SE_DIM, C), 0.008, 0.125, ((2, 8),), jnp.float32),
        "norm_m": centred(arg_keys[12], (2, 7, C), 0.1, 1.5, ((2, 8),), jnp.float32),
    }


@jax.custom_vjp
def low(v):
    return lax.optimization_barrier(v.astype(jnp.bfloat16)).astype(jnp.float32)

@jax.custom_vjp
def low_back(v):
    return v

def low_keep(v):
    return (low(v), None)

def low_pass(kept, grad):
    return (grad,)

def back_keep(v):
    return (v, None)

def back_low(kept, grad):
    return (low(grad),)
low.defvjp(low_keep, low_pass)
low_back.defvjp(back_keep, back_low)
highest = lax.Precision.HIGHEST
epsilon = 1e-05
momentum_rate = 0.9
learn_rate = 20.0
norm_rate = 0.1
weight_decay = 5e-05
trust_coef = 0.02

def live_mask(counts):
    slot_ids = jnp.arange(IMG_CAP, dtype=jnp.int32)
    living = (slot_ids[None, :] < counts[:, None]).astype(jnp.float32)
    return living.reshape(-1)[:, None, None, None]

def pointwise(activation, weight):
    return jnp.einsum('nhwc,cd->nhwd', activation, weight, precision=highest)

def grouped(activation, weight, stride):
    kernel = weight.reshape(3, 3, GW, C)
    return lax.conv_general_dilated(activation, kernel, (stride, stride), ((1, 1), (1, 1)), dimension_numbers=('NHWC', 'HWIO', 'NHWC'), feature_group_count=GROUPS, precision=highest)

def normalize(values, keep_mask, norm_gain, norm_bias, number):
    summed = lax.optimization_barrier(jnp.sum(values * keep_mask, axis=(0, 1, 2)))
    square = lax.optimization_barrier(jnp.sum(values * values * keep_mask, axis=(0, 1, 2)))
    average = summed / number
    spread = square / number - average * average
    return keep_mask * (norm_gain * ((values - average) * lax.rsqrt(spread + epsilon)) + norm_bias)

def excite_gate(normed, squeeze, excite):
    activation = jax.nn.silu(normed)
    pooled = lax.optimization_barrier(jnp.mean(activation, axis=(1, 2)))
    squeezed = jax.nn.silu(jnp.dot(pooled, squeeze, precision=highest))
    gating = jax.nn.sigmoid(jnp.dot(squeezed, excite, precision=highest))
    return activation * gating[:, None, None, :]

def conv_round(values):
    return low(low_back(values))

def branch(entry, pointwise_w, grouped_w, squeeze_w, excite_w, norm_params, keep_mask, conv_first, conv_last, layer, norm_first, stride, entry_count, outer_count):
    expanded = conv_round(pointwise(entry, low(pointwise_w[conv_first])))
    hidden = low(jax.nn.silu(normalize(expanded, keep_mask, norm_params[0, norm_first], norm_params[1, norm_first], entry_count)))
    mixed = low_back(grouped(hidden, low(grouped_w[layer]), stride))
    normed = normalize(mixed, keep_mask, norm_params[0, norm_first + 1], norm_params[1, norm_first + 1], outer_count)
    excited = low(excite_gate(normed, squeeze_w[layer], excite_w[layer]))
    narrowed = conv_round(pointwise(excited, low(pointwise_w[conv_last])))
    return normalize(narrowed, keep_mask, norm_params[0, norm_first + 2], norm_params[1, norm_first + 2], outer_count)

def forward(source, pointwise_w, grouped_w, squeeze_w, excite_w, norm_params, counts):
    keep_mask = live_mask(counts)
    live_total = jnp.sum(counts).astype(jnp.float32)
    inner_count = live_total * HI * HI
    outer_count = live_total * HO * HO
    inputs = source * keep_mask
    main_one = branch(inputs, pointwise_w, grouped_w, squeeze_w, excite_w, norm_params, keep_mask, 0, 1, 0, 0, 2, inner_count, outer_count)
    projected = conv_round(pointwise(inputs[:, ::2, ::2, :], low(pointwise_w[2])))
    side_path = normalize(projected, keep_mask, norm_params[0, 3], norm_params[1, 3], outer_count)
    middle = jax.nn.silu(main_one + side_path)
    main_two = branch(low(middle), pointwise_w, grouped_w, squeeze_w, excite_w, norm_params, keep_mask, 3, 4, 1, 4, 1, outer_count, outer_count)
    return jax.nn.silu(main_two + middle)

def lars_step(weight, moment, gradient, ratios):
    scaled_rate = ratios.reshape((-1,) + (1,) * (weight.ndim - 1))
    moment_new = momentum_rate * moment + learn_rate * scaled_rate * (gradient + weight_decay * weight)
    return (moment_new, weight - moment_new)

def squares(tensor):
    return lax.optimization_barrier(jnp.sum(tensor * tensor, axis=tuple(range(1, tensor.ndim))))

def reference(images, counts, out_grad, pointwise_w, grouped_w, squeeze_w, excite_w, norm_params, pointwise_m, grouped_m, squeeze_m, excite_m, norm_m):

    def network(source, point_in, group_in, squeeze_in, excite_in, norm_in):
        return forward(source, point_in, group_in, squeeze_in, excite_in, norm_in, counts)
    result, pullback = jax.vjp(network, images.astype(jnp.float32), pointwise_w, grouped_w, squeeze_w, excite_w, norm_params)
    grads = pullback(out_grad.astype(jnp.float32))
    activations = result.astype(jnp.bfloat16)
    input_grad = grads[0].astype(jnp.bfloat16)
    weight_list = (pointwise_w, grouped_w, squeeze_w, excite_w)
    moment_list = (pointwise_m, grouped_m, squeeze_m, excite_m)
    grad_list = grads[1:5]
    weight_norms = jnp.sqrt(jnp.concatenate([squares(tensor) for tensor in weight_list]))
    grad_norms = jnp.sqrt(jnp.concatenate([squares(tensor) for tensor in grad_list]))
    trust_ratio = trust_coef * weight_norms / (grad_norms + weight_decay * weight_norms)
    bounds = (0, 5, 7, 9, 11)
    updates = []
    for position in range(4):
        updates.append(lars_step(weight_list[position], moment_list[position], grad_list[position], trust_ratio[bounds[position]:bounds[position + 1]]))
    moment_norm = momentum_rate * norm_m + norm_rate * grads[5]
    new_norm = norm_params - moment_norm
    layer_norms = jnp.stack([weight_norms, grad_norms])
    return (activations, input_grad, layer_norms, grads[1], grads[2], grads[3], grads[4], grads[5], updates[0][0], updates[1][0], updates[2][0], updates[3][0], moment_norm, updates[0][1], updates[1][1], updates[2][1], updates[3][1], new_norm)
```

```python
import functools

import jax
import jax.numpy as jnp
import numpy as np
from jax import lax
from jax.experimental import pallas as pl
from jax.experimental.pallas import tpu as pltpu
from jax.sharding import PartitionSpec as P

GROUPS = 36
GW = 56

highest = lax.Precision.HIGHEST
epsilon = 1e-05
momentum_rate = 0.9
learn_rate = 20.0
norm_rate = 0.1
weight_decay = 5e-05
trust_coef = 0.02
bf16 = jnp.bfloat16
f32 = jnp.float32
AXES = ("rows", "chan")
NT = (((1,), (1,)), ((), ()))
NN = (((1,), (0,)), ((), ()))


def round_up(value, step):
    return (value + step - 1) // step * step


class Wire:
    def __init__(self, rows, chan):
        self.rows, self.chan = rows, chan
        self.row = lax.axis_index("rows")
        self.col = lax.axis_index("chan")
        self.deep = [
            (dr << 1, dc << 2) for dc in range(max(1, chan // 4)) for dr in range(rows // 2)
        ]
        place_r, place_c = [], []
        core = self.col & 1
        for dc in range(2):
            for second in range(2):
                for first in range(2):
                    for dr, dk in self.deep:
                        source = core ^ dc
                        dy = jnp.where(source == 0, first, second)
                        dx = jnp.where(source == 0, second, first)
                        place_r.append(self.row ^ dr ^ dy)
                        place_c.append(self.col ^ dk ^ dc ^ (dx << 1))
        self.place = jnp.stack([jnp.stack(place_r), jnp.stack(place_c)]).astype(jnp.int32)
        count = rows * chan
        self.groups = [list(range(core, count, 2)) for core in range(2)]
        index = jnp.arange(count // 2, dtype=jnp.int32) * 2
        halves = [index + core, index + (1 - core)]
        self.place_half = jnp.concatenate([jnp.stack([h // chan, h % chan]) for h in halves], axis=1)

    def swap(self, value, mask):
        pairs = []
        for device in range(self.rows * self.chan):
            r, c = device // self.chan, device % self.chan
            dr, dc = mask(c & 1) if callable(mask) else mask
            pairs.append((device, (r ^ dr) * self.chan + (c ^ dc)))
        return lax.ppermute(value, AXES, pairs)

    def first(self, value):
        return self.swap(value, lambda core: (1, 0) if core == 0 else (0, 2))

    def second(self, value):
        return self.swap(value, lambda core: (0, 2) if core == 0 else (1, 0))

    def core(self, value):
        return self.swap(value, (0, 1))

    def tree(self, parts):
        while len(parts) > 1:
            parts = [parts[i] + parts[i + 1] for i in range(0, len(parts), 2)]
        return parts[0]

    def sum_planes(self, value):
        for masks in ([(1, 0), (0, 2), (1, 2)], self.deep[1:]):
            value = self.tree([value] + [self.swap(value, mask) for mask in masks])
        return value

    def gather_half(self, shard):
        return lax.all_gather(shard, AXES, axis_index_groups=self.groups)

    def sum_chips(self, value):
        count = self.rows * self.chan
        groups = [list(range(core, count, 2)) for core in range(2)]
        copies = jnp.broadcast_to(value[None], (count // 2,) + value.shape)
        copies = lax.all_to_all(copies, AXES, 0, 0, axis_index_groups=groups, tiled=True)
        return jnp.sum(copies, axis=0)

    def trade(self, values):
        return lax.all_to_all(values, AXES, 0, 0, tiled=True)


class Gather:
    def __init__(self, wire, shard):
        self.wire, self.items, self.stage = wire, [shard], 0

    def go(self, items):
        wire, self.items = self.wire, items
        if self.stage == 0:
            self.pending = [wire.swap(items[0], mask) for mask in wire.deep[1:]]
        else:
            step = (None, wire.first, wire.second, wire.core)[self.stage]
            self.pending = [step(item) for item in items]

    def arrive(self, arrived):
        if self.stage == 0:
            self.items = [jnp.stack(self.items + arrived)]
        elif self.stage == 1:
            self.items = [jnp.concatenate(self.items + arrived)]
        else:
            self.items = self.items + arrived
        self.stage += 1


class Scatter:
    def __init__(self, wire, blocks=None, sent=None):
        self.wire, self.stage = wire, 1
        if blocks is None:
            self.items = [sent]
            return
        half = blocks.shape[0] // 2
        self.keep, self.items = blocks[:half], [blocks[half:]]
        if 2 * half == wire.rows * wire.chan:
            self.stage = 0

    def go(self, items):
        wire, self.items = self.wire, items
        if self.stage < 3:
            step = (wire.core, wire.second, wire.first)[self.stage]
            self.pending = [step(items[0])]
        else:
            self.pending = [wire.swap(item, mask) for item, mask in zip(items, wire.deep[1:])]

    def arrive(self, arrived):
        def add(a, b):
            return (a.astype(f32) + b.astype(f32)).astype(bf16)

        if self.stage < 2:
            half = self.keep.shape[0] // 2
            self.items = [add(self.keep[half:], arrived[0][half:])]
            self.keep = add(self.keep[:half], arrived[0][:half])
        elif self.stage == 2:
            parts = [add(self.keep[i], arrived[0][i]) for i in range(len(self.wire.deep))]
            self.keep, self.items = parts[0], parts[1:]
        else:
            self.total = self.wire.tree([part.astype(f32) for part in [self.keep] + arrived])
        self.stage += 1


class Pair:
    def __init__(self, wire, value):
        self.wire, self.items = wire, [value]

    def go(self, items):
        self.items, self.pending = items, [self.wire.core(items[0])]

    def arrive(self, arrived):
        self.items = self.items + arrived


def hook(value, wait=(), go=()):
    value, arrived, items = lax.optimization_barrier(
        (value, [flow.pending for flow in wait], [f.items for f in go if f not in wait])
    )
    for flow, got in zip(wait, arrived):
        flow.arrive(got)
    items = iter(items)
    for flow in go:
        flow.go(flow.items if flow in wait else next(items))
    return value


def widen(value, blocks, size):
    value = value.reshape(value.shape[:-1] + (blocks, -1))
    value = jnp.pad(value, [(0, 0)] * (value.ndim - 1) + [(0, size - value.shape[-1])])
    return value.reshape(value.shape[:-2] + (blocks * size,))


def narrow(value, blocks, size):
    value = value.reshape(value.shape[:-1] + (blocks, -1))[..., :size]
    return value.reshape(value.shape[:-2] + (blocks * size,))


def sigmoid(value):
    return 0.5 * jnp.tanh(0.5 * value) + 0.5


def silu(value):
    half = 0.5 * value
    return half * jnp.tanh(half) + half


def silu_slope(value):
    gate = sigmoid(value)
    return gate * (1.0 + value * (1.0 - gate))


def fold(value):
    return jnp.sum(value.reshape(value.shape[0] // 8, 8, value.shape[1]), axis=0)


def down(value):
    return jnp.sum(value, axis=0, keepdims=True)


def stats_of(sums, number):
    average = sums[0:1] / number
    return average, lax.rsqrt(sums[1:2] / number - average * average + epsilon)


def forward_scale(sums, norm, j, number):
    average, inverse = stats_of(sums, number)
    a = norm[j : j + 1] * inverse
    return a, norm[7 + j : 8 + j] - average * a


def backward_scale(sums, back, norm, j, number):
    average, inverse = stats_of(sums, number)
    a = norm[j : j + 1] * inverse
    c = -a * inverse * back[0:1] / number
    return a, c, -a * back[1:2] / number - c * average


def sds(shape, dtype):
    return jax.ShapeDtypeStruct(shape, dtype)


ANY = pl.BlockSpec(memory_space=pl.ANY)
VM = pl.BlockSpec(memory_space=pltpu.VMEM)
SM = pl.BlockSpec(memory_space=pltpu.SMEM)


def call(body, outs, args, specs, out_specs=None, scratch=(), grid=(), flops=0, moved=0):
    return pl.pallas_call(
        body,
        out_shape=outs,
        grid=grid,
        in_specs=specs,
        out_specs=out_specs if out_specs is not None else [VM] * len(outs),
        scratch_shapes=list(scratch),
        compiler_params=pltpu.CompilerParams(
            vmem_limit_bytes=60 * 1024 * 1024,
            dimension_semantics=("arbitrary",) * len(grid) if grid else None,
        ),
        cost_estimate=pl.CostEstimate(flops=flops, bytes_accessed=moved, transcendentals=0),
    )(*args)


def load_weight(place, pieces, dest, sem, start):
    height, width = pieces[0].shape[1:]
    count = pieces[0].shape[0]
    if not start:
        pltpu.make_async_copy(dest, dest, sem).wait()
        return
    for k, piece in enumerate(pieces):
        for i in range(count):
            p = k * count + i
            r = pl.multiple_of(place[0, p] * height, height)
            c = pl.multiple_of(place[1, p] * width, width)
            pltpu.make_async_copy(
                piece.at[i], dest.at[pl.ds(r, height), pl.ds(c, width)], sem
            ).start()


def lane_tiles(full, step, body):
    @pl.loop(0, full // step)
    def _(i):
        body(pl.ds(pl.multiple_of(i * step, step), step))


def point_kernel(place, x_ref, *rest):
    pieces, (out_ref, sums_ref, w_ref, sem) = rest[:-4], rest[-4:]

    @pl.when(pl.program_id(0) == 0)
    def _():
        load_weight(place, pieces, w_ref, sem, True)
        sums_ref[...] = jnp.zeros_like(sums_ref)
        load_weight(place, pieces, w_ref, sem, False)

    x = x_ref[...].reshape(-1, x_ref.shape[-1])

    def chunk(lanes):
        result = jnp.dot(x, w_ref[:, lanes], preferred_element_type=f32).astype(bf16)
        out_ref[..., lanes] = result.reshape(out_ref.shape[:-1] + (result.shape[1],))
        wide = result.astype(f32)
        sums_ref[0:1, lanes] += down(fold(wide))
        sums_ref[1:2, lanes] += down(fold(wide * wide))

    lane_tiles(w_ref.shape[1], 512, chunk)


def point(place, x, pieces, planes):
    slots, _, rows, full = x.shape
    spec = pl.BlockSpec((slots, 1, rows, full), lambda i: (0, i, 0, 0))
    outs = [sds((slots, planes, rows, full), bf16), sds((2, full), f32)]
    return call(
        point_kernel,
        outs,
        (place, x, *pieces),
        [SM, spec] + [ANY] * len(pieces),
        [spec, pl.BlockSpec((2, full), lambda i: (0, 0))],
        [pltpu.VMEM((full, full), bf16), pltpu.SemaphoreType.DMA],
        (planes,),
        2 * slots * planes * rows * full * full,
        full * full * 2 + 4 * slots * planes * rows * full,
    )


def weight_kernel(order, *refs):
    pairs, out_ref = refs[:-1], refs[-1]
    count, height, width = out_ref.shape
    full = pairs[0].shape[1]
    down_blocks = full // height

    @pl.loop(0, down_blocks)
    def _(r):
        rows = pl.ds(pl.multiple_of(r * height, height), height)
        turned = [x[:, rows].T for x in pairs[0::2]]
        for k in range(count // down_blocks):
            spot = order[0, r * (count // down_blocks) + k]
            c = order[1, r * (count // down_blocks) + k]
            across = pl.ds(pl.multiple_of(c * width, width), width)
            block = 0.0
            for xt, g in zip(turned, pairs[1::2]):
                block = block + jnp.dot(xt, g[:, across], preferred_element_type=f32)
            out_ref[spot] = block.astype(bf16)


def weight_grad(order, pairs, height, width):
    rows, full = pairs[0].shape
    count = order.shape[1]
    return call(
        weight_kernel,
        [sds((count, height, width), bf16)],
        (order, *pairs),
        [SM] + [VM] * len(pairs),
        flops=len(pairs) * rows * height * width * count,
        moved=count * height * width * 2 + 2 * rows * full * len(pairs),
    )[0]


def plane_weight_kernel(order, x0_ref, x1_ref, g0_ref, g1_ref, out_ref):
    count, height, width = out_ref.shape
    slots, _, rows, full = x0_ref.shape
    down_blocks = full // height
    each = count // down_blocks

    @pl.loop(0, down_blocks)
    def _(r):
        lanes = pl.ds(pl.multiple_of(r * height, height), height)
        turned = [x[:, 0, :, lanes].reshape(slots * rows, height).T for x in (x0_ref, x1_ref)]
        for k in range(each):
            across = pl.ds(pl.multiple_of(order[1, r * each + k] * width, width), width)
            block = 0.0
            for xt, g in zip(turned, (g0_ref, g1_ref)):
                block = block + jnp.dot(xt, g[:, across], preferred_element_type=f32)
            out_ref[order[0, r * each + k]] = block.astype(bf16)


def plane_weight_grad(order, x_pair, g_pair, height, width):
    slots, _, rows, full = x_pair[0].shape
    count = order.shape[1]
    x_spec = pl.BlockSpec((slots, 1, rows, full), lambda i: (0, 0, 0, 0))
    g_spec = pl.BlockSpec((slots * rows, full), lambda i: (0, 0))
    return call(
        plane_weight_kernel,
        [sds((count, height, width), bf16)],
        (order, *x_pair, *g_pair),
        [SM, x_spec, x_spec, g_spec, g_spec],
        [pl.BlockSpec((count, height, width), lambda i: (0, 0, 0))],
        (),
        (1,),
        4 * slots * rows * height * width * count,
        count * height * width * 2 + 8 * slots * rows * full,
    )[0]


def entry_weight_kernel(spots, x0_ref, x1_ref, g0_ref, g1_ref, out_ref):
    planes, rows, height = x0_ref.shape[1], x0_ref.shape[2], x0_ref.shape[3]
    depth = x0_ref.shape[0] * rows
    block = 0.0
    for x_ref, g_ref in ((x0_ref, g0_ref), (x1_ref, g1_ref)):
        for k in range(planes):
            x = x_ref[:, k].reshape(depth, height)
            block = block + jnp.dot(g_ref[k, :, 0:depth], x, preferred_element_type=f32)
    out_ref[0] = block.T.astype(bf16)


def entry_weight(spots, x_pair, g_pair, height, width):
    slots, planes, rows, full = x_pair[0].shape
    count, deep = spots.shape[1], g_pair[0].shape[2]
    x_spec = pl.BlockSpec((slots, planes, rows, height), lambda i, at: (0, 0, 0, at[0, i]))
    g_spec = pl.BlockSpec((planes, width, deep), lambda i, at: (0, at[1, i], 0))
    return pl.pallas_call(
        entry_weight_kernel,
        out_shape=[sds((count, height, width), bf16)],
        grid_spec=pltpu.PrefetchScalarGridSpec(
            num_scalar_prefetch=1,
            grid=(count,),
            in_specs=[x_spec, x_spec, g_spec, g_spec],
            out_specs=[pl.BlockSpec((1, height, width), lambda i, at: (i, 0, 0))],
        ),
        compiler_params=pltpu.CompilerParams(
            vmem_limit_bytes=60 * 1024 * 1024, dimension_semantics=("arbitrary",)
        ),
        cost_estimate=pl.CostEstimate(
            flops=4 * slots * planes * rows * height * width * count,
            bytes_accessed=4 * x_pair[0].size,
            transcendentals=0,
        ),
    )(spots, *x_pair, *g_pair)[0]


def prepare_kernel(count, select, x_ref, out_ref, rows_ref, *, blocks):
    _, high, side_in, channels = x_ref.shape
    block = channels // blocks
    lanes = out_ref.shape[-1] // blocks
    pad = rows_ref.shape[0] // high

    @pl.when((pl.program_id(0) == 0) & (pl.program_id(1) == 0))
    def _():
        rows_ref[...] = jnp.zeros_like(rows_ref)

    live = pl.program_id(0) < count[0]
    for h in range(high):
        value = x_ref[0, h]
        rows_ref[h * pad : h * pad + side_in, :] = jnp.where(live, value, jnp.zeros_like(value))
    sorted_rows = jnp.dot(select[...], rows_ref[...], preferred_element_type=f32)
    shape = out_ref.shape[1:-1]
    for r in range(blocks):
        part = sorted_rows[:, r * block : (r + 1) * block]
        part = jnp.concatenate(
            [part, jnp.zeros((part.shape[0], lanes - block), f32)], axis=1
        )
        out_ref[0, :, :, :, :, r * lanes : (r + 1) * lanes] = part.astype(bf16).reshape(
            shape + (lanes,)
        )


def parity_select(high, pad, side_in, wide):
    out = np.zeros((high * 2 * wide, high * pad), np.float32)
    for h in range(high):
        for w in range(side_in):
            target = (((h % 2) * 2 + w % 2) * (high // 2) + h // 2) * wide + w // 2
            out[target, h * pad + w] = 1.0
    return out


def prepare(count, images, blocks, lanes, wide):
    slots, side_in, _, channels = images.shape
    side, high, pad = side_in // 2, 4, 32
    select = jnp.asarray(parity_select(high, pad, side_in, wide), bf16)
    full = blocks * lanes
    return call(
        functools.partial(prepare_kernel, blocks=blocks),
        [sds((slots, 2, 2, side, wide, full), bf16)],
        (count, select, images),
        [
            SM,
            pl.BlockSpec(select.shape, lambda n, q: (0, 0)),
            pl.BlockSpec((1, high, side_in, channels), lambda n, q: (n, q, 0, 0)),
        ],
        [pl.BlockSpec((1, 2, 2, high // 2, wide, full), lambda n, q: (n, 0, 0, q, 0, 0))],
        [pltpu.VMEM((high * pad, channels), bf16)],
        (slots, side_in // high),
        moved=images.size * 4,
    )[0]


def restore_kernel(select, even_ref, odd_ref, out_ref, *, blocks):
    _, high, side_in, channels = out_ref.shape
    block = channels // blocks
    full = even_ref.shape[-1]
    lanes = full // blocks
    value = jnp.concatenate([ref[0].reshape(-1, full) for ref in (even_ref, odd_ref)], axis=0)
    rows = jnp.dot(select[...], value, preferred_element_type=f32)
    pad = rows.shape[0] // high
    joined = jnp.concatenate(
        [rows[:, r * lanes : r * lanes + block] for r in range(blocks)], axis=1
    ).astype(bf16)
    for h in range(high):
        out_ref[0, h] = joined[h * pad : h * pad + side_in]


def restore(even, odd, blocks, channels):
    slots, _, side, wide, full = even.shape
    side_in, high, pad = 2 * side, 4, 32
    select = jnp.asarray(parity_select(high, pad, side_in, wide).T, bf16)
    spec = pl.BlockSpec((1, 2, high // 2, wide, full), lambda n, q: (n, 0, q, 0, 0))
    return call(
        functools.partial(restore_kernel, blocks=blocks),
        [sds((slots, side_in, side_in, channels), bf16)],
        (select, even, odd),
        [pl.BlockSpec(select.shape, lambda n, q: (0, 0)), spec, spec],
        [pl.BlockSpec((1, high, side_in, channels), lambda n, q: (n, q, 0, 0))],
        (),
        (slots, side_in // high),
        moved=even.size * 8,
    )[0]


def widen_kernel(v_ref, out_ref, *, blocks):
    _, high, side, channels = v_ref.shape
    block = channels // blocks
    lanes = out_ref.shape[-1] // blocks
    wide = out_ref.shape[2]
    for h in range(high):
        value = v_ref[0, h].astype(f32)
        value = jnp.concatenate([value, jnp.zeros((wide - side, channels), f32)], axis=0)
        for r in range(blocks):
            part = value[:, r * block : (r + 1) * block]
            part = jnp.concatenate([part, jnp.zeros((wide, lanes - block), f32)], axis=1)
            out_ref[0, h, :, r * lanes : (r + 1) * lanes] = part.astype(bf16)


def widen_image(value, blocks, lanes, wide):
    slots, side, _, channels = value.shape
    full = blocks * lanes
    return call(
        functools.partial(widen_kernel, blocks=blocks),
        [sds((slots, side, wide, full), bf16)],
        (value,),
        [pl.BlockSpec((1, 2, side, channels), lambda n, q: (n, q, 0, 0))],
        [pl.BlockSpec((1, 2, wide, full), lambda n, q: (n, q, 0, 0))],
        (),
        (slots, side // 2),
        moved=value.size * 4,
    )[0]


def narrow_kernel(v_ref, out_ref, *, blocks):
    _, high, side, channels = out_ref.shape
    block = channels // blocks
    lanes = v_ref.shape[-1] // blocks
    for h in range(high):
        value = v_ref[0, h].astype(f32)
        joined = jnp.concatenate(
            [value[:, r * lanes : r * lanes + block] for r in range(blocks)], axis=1
        )
        out_ref[0, h] = joined[:side].astype(bf16)


def narrow_image(value, blocks, channels):
    slots, side, wide, full = value.shape
    return call(
        functools.partial(narrow_kernel, blocks=blocks),
        [sds((slots, side, side, channels), bf16)],
        (value,),
        [pl.BlockSpec((1, 2, wide, full), lambda n, q: (n, q, 0, 0))],
        [pl.BlockSpec((1, 2, side, channels), lambda n, q: (n, q, 0, 0))],
        (),
        (slots, side // 2),
        moved=value.size * 4,
    )[0]


def dense_kernel(w_ref, place_ref, same_ref, out_ref):
    for t in range(w_ref.shape[0]):
        spread = jnp.dot(place_ref[...], w_ref[t], preferred_element_type=f32)
        out_ref[t, 0] = (spread * same_ref[...].astype(f32)).astype(bf16)


def dense_grouped(weight, place, same):
    nine, part, full = weight.shape
    tile = same.shape[0]
    tiles = full // tile
    return call(
        dense_kernel,
        [sds((nine, tiles, tile, tile), bf16)],
        (weight, place, same),
        [
            pl.BlockSpec((nine, part, tile), lambda j: (0, 0, j)),
            pl.BlockSpec(place.shape, lambda j: (0, 0)),
            pl.BlockSpec(same.shape, lambda j: (0, 0)),
        ],
        [pl.BlockSpec((nine, 1, tile, tile), lambda j: (0, j, 0, 0))],
        (),
        (tiles,),
        moved=nine * full * tile * 2,
    )[0]


def tap_views(stride):
    views = []
    for a in range(3):
        for b in range(3):
            if stride == 1:
                views.append((0, 0, a - 1, b - 1))
            else:
                views.append((int(a != 1), int(b != 1), -int(a == 0), -int(b == 0)))
    return views


def fill_planes(store, a_ref, scale, offset, keep_ref, wide, stride, slope_ref=None):
    slots, planes, rows, tile = a_ref.shape
    gap = rows + wide

    @pl.when(pl.program_id(0) == 0)
    def _():
        zero = jnp.zeros(store.shape[:1] + (wide, tile), bf16)
        for n in range(slots + 1):
            if n * gap < store.shape[1]:
                store[:, n * gap : n * gap + wide, :] = zero

    def chunk(lanes):
        a, b = scale[:, lanes], offset[:, lanes]
        for n in range(slots):
            mask = keep_ref[n * rows : (n + 1) * rows, :]
            for k in range(planes):
                y = (a_ref[n, k, :, lanes].astype(f32) * a + b) * mask
                half = 0.5 * y
                t = jnp.tanh(half)
                h = half * t + half
                if slope_ref is not None:
                    slope_ref[n, k, :, lanes] = (0.5 * t + 0.5) * (1.0 + half * (1.0 - t))
                span = slice(n * gap + wide, n * gap + wide + rows)
                if stride == 1:
                    store[0, span, lanes] = pltpu.roll(h, 1, 0).astype(bf16)
                    store[1, span, lanes] = h.astype(bf16)
                    store[2, span, lanes] = pltpu.roll(h, rows - 1, 0).astype(bf16)
                else:
                    hp, wp = k // 2, k % 2
                    store[hp * 3 + wp, span, lanes] = h.astype(bf16)
                    if wp:
                        store[hp * 3 + 2, span, lanes] = pltpu.roll(h, 1, 0).astype(bf16)

    for lane in range(0, tile, 128):
        chunk(slice(lane, lane + 128))


def view_of(store, tap, stride, wide, span):
    hp, wp, dy, dx = tap
    which = dx + 1 if stride == 1 else hp * 3 + wp - dx
    start = wide + dy * wide
    return store[which, start : start + span, :]


def grouped_kernel(number, sums_ref, norm_ref, keep_ref, a_ref, dense_ref, out_ref, osum_ref,
                   store, scales, *, j, stride, wide, which):
    slots, planes, rows, tile = a_ref.shape
    scale, offset = forward_scale(sums_ref[...], norm_ref[...], j, number[which])
    scales[0:1], scales[1:2] = scale, offset
    fill_planes(store, a_ref, scales.at[0:1], scales.at[1:2], keep_ref, wide, stride)
    span = slots * rows + (slots - 1) * wide
    total = None
    for t, tap in enumerate(tap_views(stride)):
        part = jnp.dot(
            view_of(store, tap, stride, wide, span), dense_ref[t, 0], preferred_element_type=f32
        )
        total = part if total is None else total + part
    first = second = 0.0
    for n in range(slots):
        start = n * (rows + wide)
        mask = jnp.concatenate([keep_ref[n * rows : (n + 1) * rows, :]] * (tile // 128), axis=1)
        value = total[start : start + rows] * mask
        out_ref[n * rows : (n + 1) * rows, :] = value.astype(bf16)
        first = first + down(fold(value))
        second = second + down(fold(value * value))
    osum_ref[0:1], osum_ref[1:2] = first, second


def lane_block(shape, tile):
    zeros = (0,) * (len(shape) - 1)
    return pl.BlockSpec(shape[:-1] + (tile,), lambda i: zeros + (i,))


def plane_rows(stride):
    return 3 if stride == 1 else 6


def grouped_forward(number, sums, norm, keep, a, dense, j, stride, wide, which):
    slots, planes, rows, full = a.shape
    tile = dense.shape[-1]
    height = wide + slots * (rows + wide)
    return call(
        functools.partial(grouped_kernel, j=j, stride=stride, wide=wide, which=which),
        [sds((slots * rows, full), bf16), sds((2, full), f32)],
        (number, sums, norm, keep, a, dense),
        [
            SM,
            lane_block(sums.shape, tile),
            lane_block(norm.shape, tile),
            pl.BlockSpec(keep.shape, lambda i: (0, 0)),
            lane_block(a.shape, tile),
            pl.BlockSpec((9, 1, tile, tile), lambda i: (0, i, 0, 0)),
        ],
        [lane_block((slots * rows, full), tile), lane_block((2, full), tile)],
        [pltpu.VMEM((plane_rows(stride), height, tile), bf16), pltpu.VMEM((2, tile), f32)],
        (full // tile,),
        18 * slots * rows * full * tile,
        dense.size * 2 + a.size * 2,
    )


def grouped_back_kernel(number, sums_ref, norm_ref, keep_ref, a_ref, dense_ref, g_ref, c_ref,
                        csum_ref, cback_ref, place_ref, same_ref, dv_ref, back_ref, kernel_ref,
                        store, scales, grads, slope, *, j, stride, wide, which):
    slots, planes, rows, tile = a_ref.shape
    gap = rows + wide
    number_in, number_out = number[which], number[1]
    scale, offset = forward_scale(sums_ref[...], norm_ref[...], j, number_in)
    scales[0:1], scales[1:2] = scale, offset
    fill_planes(store, a_ref, scales.at[0:1], scales.at[1:2], keep_ref, wide, stride, slope)
    ga, gc, gb = backward_scale(csum_ref[...], cback_ref[...], norm_ref[...], j + 1, number_out)
    scales[2:3], scales[3:4], scales[4:5] = ga, gc, gb

    @pl.when(pl.program_id(0) == 0)
    def _():
        for n in range(slots + 1):
            grads[:, n * gap : n * gap + wide, :] = jnp.zeros((3, wide, tile), bf16)

    for lane in range(0, tile, 128):
        lanes = slice(lane, lane + 128)
        pa, pc, pb = scales[2:3, lanes], scales[3:4, lanes], scales[4:5, lanes]
        for n in range(slots):
            span = slice(n * rows, (n + 1) * rows)
            g, c = g_ref[span, lanes].astype(f32), c_ref[span, lanes].astype(f32)
            dc = (g * pa + c * pc + pb) * keep_ref[span, :]
            to = slice(n * gap + wide, n * gap + wide + rows)
            grads[1, to, lanes] = dc.astype(bf16)
            grads[2, to, lanes] = pltpu.roll(dc, rows - 1, 0).astype(bf16)
            if stride == 1:
                grads[0, to, lanes] = pltpu.roll(dc, 1, 0).astype(bf16)
    span = slots * rows + (slots - 1) * wide
    fields = {}
    for t, (hp, wp, dy, dx) in enumerate(tap_views(stride)):
        start = wide - dy * wide
        part = lax.dot_general(
            grads[1 - dx, start : start + span, :], dense_ref[t, 0], NT,
            preferred_element_type=f32,
        )
        key = hp * 2 + wp
        fields[key] = part if key not in fields else fields[key] + part
    first = second = 0.0
    average, inverse = stats_of(sums_ref[...], number_in)
    for n in range(slots):
        mask = jnp.concatenate([keep_ref[n * rows : (n + 1) * rows, :]] * (tile // 128), axis=1)
        for k in range(planes):
            dv = fields[k][n * gap : n * gap + rows] * slope[n, k] * mask
            dv_ref[n, k] = dv.astype(dv_ref.dtype)
            first = first + down(fold(dv * ((a_ref[n, k].astype(f32) - average) * inverse)))
            second = second + down(fold(dv))
    back_ref[0:1], back_ref[1:2] = first, second
    flat = grads[1, wide : wide + span, :].T
    for t, tap in enumerate(tap_views(stride)):
        dense_grad = jnp.dot(
            flat, view_of(store, tap, stride, wide, span), preferred_element_type=f32
        )
        kept = (dense_grad * same_ref[...].astype(f32)).astype(bf16)
        kernel_ref[t] = lax.dot_general(
            place_ref[...], kept, NT, preferred_element_type=f32
        ).astype(bf16)


def grouped_backward(number, sums, norm, keep, a, dense, g, c, csum, cback, place_t, same, j,
                     stride, wide, which, dtype):
    slots, planes, rows, full = a.shape
    tile = dense.shape[-1]
    part = place_t.shape[0]
    height = wide + slots * (rows + wide)
    flat = (slots * rows, full)
    return call(
        functools.partial(grouped_back_kernel, j=j, stride=stride, wide=wide, which=which),
        [sds(a.shape, dtype), sds((2, full), f32), sds((9, part, full), bf16)],
        (number, sums, norm, keep, a, dense, g, c, csum, cback, place_t, same),
        [
            SM,
            lane_block(sums.shape, tile),
            lane_block(norm.shape, tile),
            pl.BlockSpec(keep.shape, lambda i: (0, 0)),
            lane_block(a.shape, tile),
            pl.BlockSpec((9, 1, tile, tile), lambda i: (0, i, 0, 0)),
            lane_block(flat, tile),
            lane_block(flat, tile),
            lane_block(csum.shape, tile),
            lane_block(cback.shape, tile),
            pl.BlockSpec(place_t.shape, lambda i: (0, 0)),
            pl.BlockSpec(same.shape, lambda i: (0, 0)),
        ],
        [lane_block(a.shape, tile), lane_block((2, full), tile), lane_block((9, part, full), tile)],
        [
            pltpu.VMEM((plane_rows(stride), height, tile), bf16),
            pltpu.VMEM((8, tile), f32),
            pltpu.VMEM((3, height, tile), bf16),
            pltpu.VMEM((slots, planes, rows, tile), f32),
        ],
        (full // tile,),
        54 * slots * rows * full * tile,
        dense.size * 2 + a.size * 2,
    )


def split_dot(value, weight, dims):
    high = value.astype(bf16).astype(f32)
    rows = jnp.concatenate([high, value - high], axis=0).astype(bf16)
    result = lax.dot_general(rows, weight, dims, preferred_element_type=f32)
    return result[:8] + result[8:]


def excite_kernel(number, place, sums_ref, norm_ref, keep_ref, c_ref, sq_ref, ex_ref, *rest,
                  j, slots, pixels):
    pieces, rest = rest[:-11], rest[-11:]
    e_ref, a_ref, osum_ref, pool_ref, gate_ref, pre_ref, q_ref, w_ref, sem, hold, scales = rest
    load_weight(place, pieces, w_ref, sem, True)
    scales[0:1], scales[1:2] = forward_scale(sums_ref[...], norm_ref[...], j, number[1])
    rows, full = c_ref.shape
    each = rows // slots
    pool_ref[...] = jnp.zeros_like(pool_ref)

    def pass_one(lanes):
        a, b = scales[0:1, lanes], scales[1:2, lanes]
        for n in range(slots):
            span = slice(n * each, (n + 1) * each)
            h = silu((c_ref[span, lanes].astype(f32) * a + b) * keep_ref[span, :])
            hold[span, lanes] = h
            pool_ref[n : n + 1, lanes] = down(fold(h)) * (1.0 / pixels)

    lane_tiles(full, 128, pass_one)
    pre = split_dot(pool_ref[...], sq_ref[...], NT)
    q = silu(pre)
    pre_ref[...], q_ref[...] = pre, q
    gate_ref[...] = sigmoid(split_dot(q, ex_ref[...], NN))

    def pass_two(lanes):
        for n in range(slots):
            span = slice(n * each, (n + 1) * each)
            e_ref[span, lanes] = (hold[span, lanes] * gate_ref[n : n + 1, lanes]).astype(bf16)

    lane_tiles(full, 128, pass_two)
    load_weight(place, pieces, w_ref, sem, False)
    matmul_sums(e_ref, w_ref, a_ref, osum_ref)


def matmul_sums(x_ref, w_ref, out_ref, sums_ref):
    def chunk(lanes):
        result = jnp.dot(x_ref[...], w_ref[:, lanes], preferred_element_type=f32).astype(bf16)
        out_ref[:, lanes] = result
        wide = result.astype(f32)
        sums_ref[0:1, lanes] = down(fold(wide))
        sums_ref[1:2, lanes] = down(fold(wide * wide))

    lane_tiles(w_ref.shape[1], 512, chunk)


def weight_scratch(full):
    return [pltpu.VMEM((full, full), bf16), pltpu.SemaphoreType.DMA]


def excite_forward(number, place, sums, norm, keep, c, sq, ex, pieces, j, slots, pixels):
    rows, full = c.shape
    se = sq.shape[0]
    return call(
        functools.partial(excite_kernel, j=j, slots=slots, pixels=pixels),
        [
            sds((rows, full), bf16),
            sds((rows, full), bf16),
            sds((2, full), f32),
            sds((8, full), f32),
            sds((8, full), f32),
            sds((8, se), f32),
            sds((8, se), f32),
        ],
        (number, place, sums, norm, keep, c, sq, ex, *pieces),
        [SM, SM, VM, VM, VM, VM, VM, VM] + [ANY] * len(pieces),
        scratch=weight_scratch(full)
        + [pltpu.VMEM((rows, full), f32), pltpu.VMEM((8, full), f32)],
        flops=2 * rows * full * full,
        moved=full * full * 2 + rows * full * 8,
    )


def join_kernel(number, place, sum2_ref, sum3_ref, norm_ref, keep_ref, a_ref, s_ref, *rest):
    pieces, rest = rest[:-7], rest[-7:]
    z_ref, m_ref, out_ref, osum_ref, w_ref, sem, scales = rest
    load_weight(place, pieces, w_ref, sem, True)
    scales[0:1], scales[1:2] = forward_scale(sum2_ref[...], norm_ref[...], 2, number[1])
    scales[2:3], scales[3:4] = forward_scale(sum3_ref[...], norm_ref[...], 3, number[1])

    def chunk(lanes):
        z = (
            a_ref[:, lanes].astype(f32) * scales[0:1, lanes]
            + s_ref[:, lanes].astype(f32) * scales[2:3, lanes]
            + (scales[1:2, lanes] + scales[3:4, lanes])
        ) * keep_ref[...]
        z_ref[:, lanes] = z.astype(bf16)
        m_ref[:, lanes] = silu(z).astype(bf16)

    lane_tiles(a_ref.shape[1], 128, chunk)
    load_weight(place, pieces, w_ref, sem, False)
    matmul_sums(m_ref, w_ref, out_ref, osum_ref)


def join_forward(number, place, sum2, sum3, norm, keep, a, s, pieces):
    rows, full = a.shape
    return call(
        join_kernel,
        [
            sds((rows, full), bf16),
            sds((rows, full), bf16),
            sds((rows, full), bf16),
            sds((2, full), f32),
        ],
        (number, place, sum2, sum3, norm, keep, a, s, *pieces),
        [SM, SM, VM, VM, VM, VM, VM, VM] + [ANY] * len(pieces),
        scratch=weight_scratch(full) + [pltpu.VMEM((8, full), f32)],
        flops=2 * rows * full * full,
        moved=full * full * 2 + rows * full * 8,
    )


def turn_kernel(number, sums_ref, norm_ref, keep_ref, a_ref, z_ref, g_ref, act_ref, d_ref,
                back_ref, scales):
    scales[0:1], scales[1:2] = forward_scale(sums_ref[...], norm_ref[...], 6, number[1])
    scales[2:3], scales[3:4] = stats_of(sums_ref[...], number[1])

    def chunk(lanes):
        a = a_ref[:, lanes].astype(f32)
        z = (a * scales[0:1, lanes] + scales[1:2, lanes]) * keep_ref[...]
        z = z + silu(z_ref[:, lanes].astype(f32))
        half = 0.5 * z
        t = jnp.tanh(half)
        act_ref[:, lanes] = (half * t + half).astype(bf16)
        d = g_ref[:, lanes].astype(f32) * ((0.5 * t + 0.5) * (1.0 + half * (1.0 - t)))
        d_ref[:, lanes] = d.astype(bf16)
        dz = d * keep_ref[...]
        scaled = (a - scales[2:3, lanes]) * scales[3:4, lanes]
        back_ref[0:1, lanes] = down(fold(dz * scaled))
        back_ref[1:2, lanes] = down(fold(dz))

    lane_tiles(a_ref.shape[1], 128, chunk)


def turn(number, sums, norm, keep, a, z, g):
    rows, full = a.shape
    return call(
        turn_kernel,
        [sds((rows, full), bf16), sds((rows, full), bf16), sds((2, full), f32)],
        (number, sums, norm, keep, a, z, g),
        [SM] + [VM] * 6,
        scratch=[pltpu.VMEM((8, full), f32)],
        moved=rows * full * 14,
    )


def norm_back_pass(d_ref, a_ref, keep_ref, scales, out_ref):
    def chunk(lanes):
        out_ref[:, lanes] = (
            (
                d_ref[:, lanes].astype(f32) * scales[0:1, lanes]
                + a_ref[:, lanes].astype(f32) * scales[1:2, lanes]
                + scales[2:3, lanes]
            )
            * keep_ref[...]
        ).astype(bf16)

    lane_tiles(a_ref.shape[1], 128, chunk)


def excite_back_kernel(number, place, sums_ref, back_ref, csum_ref, norm_ref, keep_ref, d_ref,
                       a_ref, c_ref, sq_ref, ex_ref, gate_ref, pre_ref, *rest, j, slots, pixels):
    pieces, rest = rest[:-10], rest[-10:]
    da_ref, du_ref, oback_ref, dgate_ref, dpre_ref, w_ref, sem, hold, scales, pool = rest
    load_weight(place, pieces, w_ref, sem, True)
    rows, full = a_ref.shape
    each = rows // slots
    scales[0:1], scales[1:2], scales[2:3] = backward_scale(
        sums_ref[...], back_ref[...], norm_ref[...], j + 1, number[1]
    )
    scales[3:4], scales[4:5] = forward_scale(csum_ref[...], norm_ref[...], j, number[1])
    scales[5:6], scales[6:7] = stats_of(csum_ref[...], number[1])
    norm_back_pass(d_ref, a_ref, keep_ref, scales, da_ref)
    dgate_ref[...] = jnp.zeros_like(dgate_ref)
    load_weight(place, pieces, w_ref, sem, False)

    def chunk(lanes):
        de = lax.dot_general(da_ref[...], w_ref[lanes, :], NT, preferred_element_type=f32)
        hold[:, lanes] = de

    lane_tiles(full, 512, chunk)

    def gates(lanes):
        a, b = scales[3:4, lanes], scales[4:5, lanes]
        for n in range(slots):
            span = slice(n * each, (n + 1) * each)
            h = silu((c_ref[span, lanes].astype(f32) * a + b) * keep_ref[span, :])
            dgate_ref[n : n + 1, lanes] = down(fold(hold[span, lanes] * h))

    lane_tiles(full, 128, gates)
    gate = gate_ref[...]
    d_gate = dgate_ref[...] * gate * (1.0 - gate)
    dgate_ref[...] = d_gate
    d_pre = split_dot(d_gate, ex_ref[...], NT) * silu_slope(pre_ref[...])
    dpre_ref[...] = d_pre
    pool[...] = split_dot(d_pre, sq_ref[...], NN) * (1.0 / pixels)

    def finish(lanes):
        a, b = scales[3:4, lanes], scales[4:5, lanes]
        first = second = 0.0
        for n in range(slots):
            span = slice(n * each, (n + 1) * each)
            c = c_ref[span, lanes].astype(f32)
            slope = silu_slope((c * a + b) * keep_ref[span, :])
            dh = hold[span, lanes] * gate_ref[n : n + 1, lanes] + pool[n : n + 1, lanes]
            du = dh * slope * keep_ref[span, :]
            du_ref[span, lanes] = du.astype(bf16)
            first = first + down(fold(du * ((c - scales[5:6, lanes]) * scales[6:7, lanes])))
            second = second + down(fold(du))
        oback_ref[0:1, lanes], oback_ref[1:2, lanes] = first, second

    lane_tiles(full, 128, finish)


def excite_backward(number, place, sums, back, csum, norm, keep, d, a, c, sq, ex, gate, pre,
                    pieces, j, slots, pixels):
    rows, full = a.shape
    se = sq.shape[0]
    return call(
        functools.partial(excite_back_kernel, j=j, slots=slots, pixels=pixels),
        [
            sds((rows, full), bf16),
            sds((rows, full), bf16),
            sds((2, full), f32),
            sds((8, full), f32),
            sds((8, se), f32),
        ],
        (number, place, sums, back, csum, norm, keep, d, a, c, sq, ex, gate, pre, *pieces),
        [SM, SM] + [VM] * 12 + [ANY] * len(pieces),
        scratch=weight_scratch(full)
        + [
            pltpu.VMEM((rows, full), f32),
            pltpu.VMEM((8, full), f32),
            pltpu.VMEM((8, full), f32),
        ],
        flops=2 * rows * full * full,
        moved=full * full * 2 + rows * full * 16,
    )


def join_back_kernel(number, place, sums_ref, back_ref, sum2_ref, sum3_ref, norm_ref, keep_ref,
                     d_ref, a_ref, skip_ref, z_ref, a3_ref, s_ref, *rest):
    pieces, rest = rest[:-7], rest[-7:]
    da_ref, dz_ref, oback_ref, w_ref, sem, scales, hold = rest
    load_weight(place, pieces, w_ref, sem, True)
    scales[0:1], scales[1:2], scales[2:3] = backward_scale(
        sums_ref[...], back_ref[...], norm_ref[...], 4, number[1]
    )
    scales[3:4], scales[4:5] = stats_of(sum2_ref[...], number[1])
    scales[5:6], scales[6:7] = stats_of(sum3_ref[...], number[1])
    norm_back_pass(d_ref, a_ref, keep_ref, scales, da_ref)
    load_weight(place, pieces, w_ref, sem, False)

    def chunk(lanes):
        dm = lax.dot_general(da_ref[...], w_ref[lanes, :], NT, preferred_element_type=f32)
        hold[:, lanes] = dm

    lane_tiles(a_ref.shape[1], 512, chunk)

    def finish(lanes):
        dm = hold[:, lanes] + skip_ref[:, lanes].astype(f32)
        dz = dm * silu_slope(z_ref[:, lanes].astype(f32)) * keep_ref[...]
        dz_ref[:, lanes] = dz.astype(bf16)
        scaled2 = (a3_ref[:, lanes].astype(f32) - scales[3:4, lanes]) * scales[4:5, lanes]
        scaled3 = (s_ref[:, lanes].astype(f32) - scales[5:6, lanes]) * scales[6:7, lanes]
        oback_ref[0:1, lanes] = down(fold(dz * scaled2))
        oback_ref[1:2, lanes] = down(fold(dz))
        oback_ref[2:3, lanes] = down(fold(dz * scaled3))

    lane_tiles(a_ref.shape[1], 128, finish)


def join_backward(number, place, sums, back, sum2, sum3, norm, keep, d, a, skip, z, a3, s,
                  pieces):
    rows, full = a.shape
    return call(
        join_back_kernel,
        [sds((rows, full), bf16), sds((rows, full), bf16), sds((3, full), f32)],
        (number, place, sums, back, sum2, sum3, norm, keep, d, a, skip, z, a3, s, *pieces),
        [SM, SM] + [VM] * 12 + [ANY] * len(pieces),
        scratch=weight_scratch(full)
        + [pltpu.VMEM((8, full), f32), pltpu.VMEM((rows, full), f32)],
        flops=2 * rows * full * full,
        moved=full * full * 2 + rows * full * 20,
    )


def side_kernel(number, place, sums_ref, back_ref, norm_ref, keep_ref, d_ref, a_ref, *rest):
    pieces, rest = rest[:-5], rest[-5:]
    da_ref, dx_ref, w_ref, sem, scales = rest
    load_weight(place, pieces, w_ref, sem, True)
    scales[0:1], scales[1:2], scales[2:3] = backward_scale(
        sums_ref[...], back_ref[...], norm_ref[...], 3, number[1]
    )
    norm_back_pass(d_ref, a_ref, keep_ref, scales, da_ref)
    load_weight(place, pieces, w_ref, sem, False)

    def chunk(lanes):
        dx_ref[:, lanes] = lax.dot_general(
            da_ref[...], w_ref[lanes, :], NT, preferred_element_type=f32
        ).astype(bf16)

    lane_tiles(a_ref.shape[1], 512, chunk)


def side_backward(number, place, sums, back, norm, keep, d, a, pieces):
    rows, full = a.shape
    return call(
        side_kernel,
        [sds((rows, full), bf16), sds((rows, full), bf16)],
        (number, place, sums, back, norm, keep, d, a, *pieces),
        [SM, SM] + [VM] * 6 + [ANY] * len(pieces),
        scratch=weight_scratch(full) + [pltpu.VMEM((8, full), f32)],
        flops=2 * rows * full * full,
        moved=full * full * 2 + rows * full * 12,
    )


def entry_norm_kernel(number, sums_ref, back_ref, norm_ref, keep_ref, d_ref, a_ref, da_ref,
                      turn_ref, scales):
    scales[0:1], scales[1:2], scales[2:3] = backward_scale(
        sums_ref[...], back_ref[...], norm_ref[...], 0, number[0]
    )
    slots, _, rows, full = d_ref.shape

    def chunk(lanes):
        d = d_ref[:, :, :, lanes].reshape(slots * rows, 128).astype(f32)
        a = a_ref[:, :, :, lanes].reshape(slots * rows, 128).astype(f32)
        da = (d * scales[0:1, lanes] + a * scales[1:2, lanes] + scales[2:3, lanes]) * keep_ref[...]
        da = da.astype(bf16)
        da_ref[:, :, :, lanes] = da.reshape(slots, 1, rows, 128)
        spare = jnp.zeros((128, turn_ref.shape[2] - slots * rows), bf16)
        turn_ref[0, lanes, :] = jnp.concatenate([da.T, spare], axis=1)

    lane_tiles(full, 128, chunk)


def entry_norm(number, sums, back, norm, keep, d, a):
    slots, planes, rows, full = a.shape
    spec = pl.BlockSpec((slots, 1, rows, full), lambda i: (0, i, 0, 0))
    whole = lambda v: pl.BlockSpec(v.shape, lambda i: (0, 0))
    deep = round_up(slots * rows, 128)
    return call(
        entry_norm_kernel,
        [sds(a.shape, bf16), sds((planes, full, deep), bf16)],
        (number, sums, back, norm, keep, d, a),
        [SM, whole(sums), whole(back), whole(norm), whole(keep), spec, spec],
        [spec, pl.BlockSpec((1, full, deep), lambda i: (i, 0, 0))],
        [pltpu.VMEM((8, full), f32)],
        (planes,),
        moved=a.size * 8,
    )


def entry_kernel(place, da_ref, side_ref, *rest, odd):
    pieces, rest = rest[:-3], rest[-3:]
    dx_ref, w_ref, sem = rest

    @pl.when(pl.program_id(0) == 0)
    def _():
        load_weight(place, pieces, w_ref, sem, True)
        load_weight(place, pieces, w_ref, sem, False)

    slots, _, rows, full = da_ref.shape
    da = da_ref[...].reshape(-1, full)
    extra = (pl.program_id(0) == 0).astype(f32)

    def chunk(lanes):
        dx = lax.dot_general(da, w_ref[lanes, :], NT, preferred_element_type=f32)
        if not odd:
            dx = dx + side_ref[:, lanes].astype(f32) * extra
        dx_ref[..., lanes] = dx.astype(bf16).reshape(dx_ref.shape[:-1] + (dx.shape[1],))

    lane_tiles(full, 512, chunk)


def entry_backward(place, da, side, pieces, odd):
    slots, planes, rows, full = da.shape
    half = planes // 2
    read = pl.BlockSpec((slots, 1, rows, full), lambda i: (0, i + half * odd, 0, 0))
    spec = pl.BlockSpec((slots, 1, rows, full), lambda i: (0, i, 0, 0))
    return call(
        functools.partial(entry_kernel, odd=odd),
        [sds((slots, half, rows, full), bf16)],
        (place, da, side, *pieces),
        [SM, read, pl.BlockSpec(side.shape, lambda i: (0, 0))] + [ANY] * len(pieces),
        [spec],
        weight_scratch(full),
        (half,),
        da.size * full,
        full * full * 2 + da.size * 2,
    )[0]


def collect_kernel(place, *refs):
    pieces, (sq_ref, ex_ref, gr_ref, more_ref) = refs[:-4], refs[-4:]
    each = sq_ref.shape[1]
    count, groups, sixteen, lanes = pieces[0].shape
    last = 2 * each + 9
    for k, piece in enumerate(pieces):
        for i in range(count):
            p = k * count + i
            across = pl.ds(pl.multiple_of(place[0, p] * lanes, lanes), lanes)
            c = place[1, p]
            sq_ref[c, :, :, across] = piece[i, 0:each]
            ex_ref[c, :, :, across] = piece[i, each : 2 * each]
            part = pl.ds(pl.multiple_of(c * sixteen, sixteen), sixteen)
            gr_ref[:, part, across] = piece[i, 2 * each : last]
            if groups > last:
                more_ref[:, :, across] = piece[i, last:]


def collect(place, pieces, chan, se_groups, full):
    _, groups, sixteen, _ = pieces[0].shape
    more = max(1, groups - 2 * se_groups - 9)
    return call(
        collect_kernel,
        [
            sds((chan, se_groups, sixteen, full), bf16),
            sds((chan, se_groups, sixteen, full), bf16),
            sds((9, chan * sixteen, full), bf16),
            sds((more, sixteen, full), bf16),
        ],
        (place, *pieces),
        [SM] + [VM] * len(pieces),
        moved=12 * 1024 * 1024,
    )


def deal_kernel(place, value_ref, out_ref):
    count, _, height, lanes = out_ref.shape
    for p in range(count):
        across = pl.ds(pl.multiple_of(place[0, p] * lanes, lanes), lanes)
        part = pl.ds(pl.multiple_of(place[1, p] * height, height), height)
        out_ref[p] = value_ref[:, part, across]


def deal(place, value, height, lanes):
    nine, part, full = value.shape
    count = part * full // (height * lanes)
    return call(
        deal_kernel,
        [sds((count, nine, height, lanes), bf16)],
        (place, value),
        [SM, VM],
        moved=value.size * 4,
    )[0]


def per_device(
    images,
    counts,
    out_grad,
    pointwise_w,
    grouped_w,
    squeeze_w,
    excite_w,
    norm_params,
    pointwise_m,
    grouped_m,
    squeeze_m,
    excite_m,
    norm_m,
):
    rows, chan = lax.axis_size("rows"), lax.axis_size("chan")
    wire = Wire(rows, chan)
    slots, side_in = images.shape[0], images.shape[1]
    side = out_grad.shape[1]
    wide = round_up(side, 16)
    block = norm_params.shape[2]
    lanes = round_up(block, 128)
    full = rows * lanes
    per_chan = rows // chan
    se = squeeze_w.shape[2]
    se_block = se // chan
    se_wide = 512 // chan
    se_full = chan * se_wide
    gw_part = GW // chan
    gw_wide = round_up(gw_part, 16)
    image = side * wide
    pixels = side * side

    index = wire.row * chan + wire.col
    own_count = lax.dynamic_index_in_dim(counts, index, keepdims=False)
    live = jnp.arange(slots, dtype=jnp.int32) < own_count
    valid = jnp.arange(wide, dtype=jnp.int32) < side
    keep = live[:, None, None] & valid[None, None, :]
    keep = jnp.broadcast_to(keep, (slots, side, wide)).reshape(slots * image, 1)
    keep = jnp.broadcast_to(keep.astype(f32), (slots * image, 128))
    live_total = jnp.sum(counts).astype(f32)
    number = jnp.stack([live_total * side_in * side_in, live_total * pixels])
    place = wire.place
    spots = jnp.arange(rows * chan, dtype=jnp.int32)

    def order_of(wanted):
        key = (place[0] * chan + place[1])[None]
        spot = jnp.sum(jnp.where(key == wanted[:, None], spots[None], 0), axis=1)
        return jnp.stack([spot, wanted % chan]).astype(jnp.int32)

    order_all = order_of(spots)
    order_core = order_of(spots[: rows * chan // 2] * 2 + (wire.col & 1))

    shards = widen(pointwise_w.astype(bf16), per_chan, lanes)
    shards = jnp.pad(shards, ((0, 0), (0, lanes - block), (0, 0)))

    def part_of(value, axis, size):
        return lax.dynamic_slice_in_dim(value, wire.col * size, size, axis)

    squeeze_part = jnp.swapaxes(part_of(squeeze_w, 2, se_block), 1, 2)
    excite_part = part_of(excite_w, 1, se_block)
    grouped_part = part_of(grouped_w, 2, gw_part)
    pad_lane = (0, lanes - block)
    squeeze_part = jnp.pad(squeeze_part, ((0, 0), (0, se_wide - se_block), pad_lane))
    excite_part = jnp.pad(excite_part, ((0, 0), (0, se_wide - se_block), pad_lane))
    grouped_part = jnp.pad(grouped_part, ((0, 0), (0, 0), (0, gw_wide - gw_part), pad_lane))
    small_shard = jnp.concatenate(
        [squeeze_part, excite_part, grouped_part.reshape(2, 9 * gw_wide, lanes)], axis=1
    ).astype(bf16)
    small_shard = small_shard.reshape(2, -1, 16, lanes)
    norm_rest = jnp.pad(norm_params.reshape(14, block), ((0, 2), pad_lane))
    norm_terms = []
    for _ in range(3):
        term = lax.reduce_precision(norm_rest, 8, 7)
        norm_terms.append(term.astype(bf16))
        norm_rest = norm_rest - term
    small_shard1 = jnp.concatenate([small_shard[0], jnp.stack(norm_terms)])

    fetch0, fetch1, fetch3 = [Gather(wire, shards[k]) for k in (0, 1, 3)]
    small2 = Gather(wire, small_shard[1])
    index_all = jnp.arange(rows * chan, dtype=jnp.int32)
    place_all = jnp.stack([index_all // chan, index_all % chan])

    def unpack(where, pieces):
        sq, ex, gr, extra = collect(where, pieces, chan, se_wide // 16, full)
        return (
            sq.reshape(se_full, full),
            ex.reshape(se_full, full),
            gr.reshape(9, chan * gw_wide, full),
            extra,
        )

    tile = 9 * GW // block * lanes
    position = np.arange(tile)
    inside = position % lanes
    channel = position // lanes * block + inside
    good = inside < block
    group = np.where(good, channel // GW, -1)
    within = channel % GW
    slot = within // gw_part * gw_wide + within % gw_part
    spread = (slot[:, None] == np.arange(chan * gw_wide)[None]) & good[:, None]
    same = jnp.asarray((group[:, None] == group[None]) & good[:, None], bf16)
    spread_t, spread = jnp.asarray(spread.T, bf16), jnp.asarray(spread, bf16)

    width = per_chan * lanes

    def both_cores(x_own, x_other, g_own, g_other):
        return weight_grad(order_core, (x_own, g_own, x_other, g_other), lanes, width)

    def sum_all(value, go=(), wait=(), beside=None, uses=()):
        value = value + wire.core(value)
        value, uses = hook((value, uses), go=go)
        if beside is None:
            value = wire.sum_planes(value)
            return hook(value, wait=wait) if wait else value
        value = wire.sum_chips(value)
        return hook((value, beside(*uses)), wait=wait)

    def vectors_of(pool, dgate, q, dpre):
        split = [
            v[:slots].reshape(slots, rows, lanes).transpose(1, 0, 2) for v in (pool, dgate)
        ]
        whole = [jnp.broadcast_to(v[:slots], (rows,) + v[:slots].shape) for v in (q, dpre)]
        sent = jnp.concatenate(split + whole, axis=2)
        sent = jnp.repeat(sent, chan, axis=0)
        return sent

    small1 = [lax.all_gather(small_shard1, AXES)]
    fetch0.go(fetch0.items)
    x = prepare(own_count[None], images, rows, lanes, wide).reshape(slots, 4, image, full)
    x, out_grad = hook((x, out_grad), (fetch0,), (fetch0,))
    gout = widen_image(out_grad, rows, lanes, wide).reshape(slots * image, full)
    x, gout = hook((x, gout), (fetch0,), (fetch0, fetch1))
    x = hook(x, (fetch0, fetch1), (fetch0, fetch1))
    place1, x = lax.optimization_barrier((place_all, x))
    sq1, ex1, gr1, norm_terms = unpack(place1, small1)
    dense1 = dense_grouped(gr1, spread, same)
    x, dense1, shard2 = hook((x, dense1, shards[2]), (fetch0, fetch1), (fetch1, fetch3))
    weight2 = Pair(wire, wire.gather_half(shard2))
    a1, sum0 = point(place, x, fetch0.items, 4)
    sum0 = hook(sum0, (fetch1, fetch3))
    sum0 = sum_all(sum0, go=(fetch1,), wait=(fetch1,))
    norm = jnp.sum(norm_terms.astype(f32), axis=0)[:14]
    sum0, shard4 = hook((sum0, shards[4]), go=(fetch3, small2))
    weight4 = Pair(wire, wire.gather_half(shard4))
    place_half = wire.place_half
    c1, sum1 = grouped_forward(number, sum0, norm, keep, a1, dense1, 0, 2, wide, 0)
    sum1 = hook(sum1, (fetch3, small2))
    sum1 = sum_all(sum1)
    sum1 = hook(sum1, go=(small2, fetch3, weight2))
    e1, a3, sum2, pool1, gate1, pre1, q1 = excite_forward(
        number, place, sum1, norm, keep, c1, sq1, ex1, fetch1.items, 1, slots, pixels
    )
    side_x, sum2 = hook((x, sum2), (weight2,))
    s1, sum3 = point(place_half, side_x, weight2.items, 1)
    s1 = s1.reshape(slots * image, full)
    sums = hook(jnp.concatenate([sum2, sum3]), (small2, fetch3))
    sums = sum_all(sums, go=(fetch3,), wait=(fetch3,))
    e1_pair = Pair(wire, e1)
    sums = hook(sums, go=(small2, e1_pair))
    sum2, sum3 = sums[:2], sums[2:]
    z1, m16, a4, sum4 = join_forward(
        number, place, sum2, sum3, norm, keep, a3, s1, fetch3.items
    )
    sum4 = hook(sum4, (small2, e1_pair))
    sum4 = sum4 + wire.core(sum4)
    sum4 = hook(sum4, go=(small2,))
    place2 = hook(place, (small2,))
    sq2, ex2, gr2, _ = unpack(place2, small2.items)
    dense2 = dense_grouped(gr2, spread, same)
    m16_pair = Pair(wire, m16)
    sum4, dense2 = hook((wire.sum_chips(sum4), dense2), go=(m16_pair, weight4))
    a4 = a4.reshape(slots, 1, image, full)
    c2, sum5 = grouped_forward(number, sum4, norm, keep, a4, dense2, 4, 1, wide, 1)
    sum5 = hook(sum5, (m16_pair, weight4))
    sum5 = sum_all(sum5)
    e2, a5, sum6, pool2, gate2, pre2, q2 = excite_forward(
        number, place_half, sum5, norm, keep, c2, sq2, ex2, weight4.items, 5, slots, pixels
    )
    sum6 = sum_all(sum6)
    e2_pair = Pair(wire, e2)
    sum6 = hook(sum6, go=(e2_pair,))
    act, d2, back6 = turn(number, sum6, norm, keep, a5, z1, gout)
    back6 = hook(back6, (e2_pair,))
    back6, activations = sum_all(
        back6,
        beside=lambda wide_act: narrow_image(
            wide_act.reshape(slots, side, wide, full), rows, images.shape[3]
        ),
        uses=(act,),
    )
    x_pair = Pair(wire, x)
    back6 = hook(back6, go=(x_pair,))
    da5, du2, back5, dgate2, dpre2 = excite_backward(
        number, place_half, sum6, back6, sum5, norm, keep, d2, a5, c2, sq2, ex2, gate2, pre2,
        weight4.items, 5, slots, pixels
    )
    back5 = hook(back5, (x_pair,))
    da5_pair = Pair(wire, da5)
    back5 = sum_all(back5, go=(da5_pair,), wait=(da5_pair,))
    dv2, back4, kernel2 = grouped_backward(
        number, sum4, norm, keep, a4, dense2, du2, c2, sum5, back5, spread_t, same, 4, 1, wide,
        1, bf16
    )
    back4, grad4 = sum_all(back4, beside=both_cores, uses=e2_pair.items + da5_pair.items)
    flow4 = Scatter(wire, grad4)
    back4 = hook(back4, go=(flow4,))
    flat4 = a4.reshape(slots * image, full)
    da4, dz1, back23 = join_backward(
        number, place, sum4, back4, sum2, sum3, norm, keep, dv2.reshape(slots * image, full),
        flat4, d2, z1, a3, s1, fetch3.items
    )
    back23 = hook(back23, (flow4,))
    da4_pair = Pair(wire, da4)
    back23 = sum_all(back23, go=(da4_pair,), wait=(da4_pair,))
    flow6 = Scatter(wire, deal(place, kernel2, gw_wide, lanes))
    back23 = hook(back23, go=(flow4, flow6))
    back2, back3 = back23[:2], jnp.stack([back23[2], back23[1]])
    da3, du1, back1, dgate1, dpre1 = excite_backward(
        number, place, sum2, back2, sum1, norm, keep, dz1, a3, c1, sq1, ex1, gate1, pre1,
        fetch1.items, 1, slots, pixels
    )
    back1 = hook(back1, (flow4, flow6))
    da3_pair = Pair(wire, da3)
    back1, grad3 = sum_all(
        back1,
        go=(da3_pair,),
        wait=(da3_pair,),
        beside=both_cores,
        uses=m16_pair.items + da4_pair.items,
    )
    flow3 = Scatter(wire, grad3)
    back1 = hook(back1, go=(flow3, flow6, flow4))
    grad1 = both_cores(*e1_pair.items, *da3_pair.items)
    flow1 = Scatter(wire, grad1)
    back1, pool1 = hook((back1, pool1), go=(flow1,))
    sent = [vectors_of(pool1, dgate1, q1, dpre1), vectors_of(pool2, dgate2, q2, dpre2)]
    vectors = wire.trade(jnp.concatenate(sent, axis=2)).reshape(rows * chan * slots, -1)
    dv1, back0, kernel1 = grouped_backward(
        number, sum0, norm, keep, a1, dense1, du1, c1, sum1, back1, spread_t, same, 0, 2, wide,
        0, bf16
    )
    back0, vectors = hook((back0, vectors), (flow3, flow6, flow4, flow1))
    back0, ((ds1, dside), deal1) = sum_all(
        back0,
        beside=lambda dz, k: (
            side_backward(number, place_half, sum3, back3, norm, keep, dz, s1, weight2.items),
            deal(place, k, gw_wide, lanes),
        ),
        uses=(dz1, kernel1),
    )
    ds1_pair, flow7 = Pair(wire, ds1), Scatter(wire, deal1)
    back0 = hook(back0, go=(ds1_pair, flow3, flow1, flow6, flow7))
    da1, da1_turned = entry_norm(number, sum0, back0, norm, keep, dv1, a1)
    da1_pair = Pair(wire, da1_turned)
    da1, dside = hook((da1, dside), (ds1_pair, flow3, flow6, flow7), (da1_pair, flow7, flow3))
    grad2 = plane_weight_grad(order_core, x_pair.items, ds1_pair.items, lanes, width)
    flow2 = Scatter(wire, grad2)
    da1, dside = hook((da1, dside), (flow1, flow7), (flow2,))
    dx_even = entry_backward(place, da1, dside, fetch0.items, 0)
    dx_even, dside, place = hook((dx_even, dside, place), (da1_pair, flow3), (flow1, flow7))
    quarter = rows * chan // 4
    sent0 = entry_weight(place[:, quarter : 2 * quarter], x_pair.items, da1_pair.items, lanes, width)
    flow0 = Scatter(wire, sent=sent0)
    place0 = hook(place, (flow2, flow7), (flow0, flow2))
    flow0.keep = entry_weight(place0[:, :quarter], x_pair.items, da1_pair.items, lanes, width)
    _, da1 = lax.optimization_barrier((flow0.keep, da1))
    dx_odd = entry_backward(place, da1, dside, fetch0.items, 1)
    dx_odd, dx_even = hook((dx_odd, dx_even), (flow0, flow1, flow2), (flow0, flow2))
    shape = (slots, 2, side, wide, full)
    input_grad = restore(dx_even.reshape(shape), dx_odd.reshape(shape), rows, images.shape[3])
    _, (vectors, totals) = hook(
        (input_grad, (vectors, [flow.total for flow in (flow1, flow3, flow4)])),
        (flow0, flow2),
        (flow0, flow6, flow7),
    )
    flow1.total, flow3.total, flow4.total = totals
    vectors = hook(vectors, (flow6, flow7))
    half = vectors.shape[1] // 2
    vectors1, vectors2 = vectors[:, :half], vectors[:, half:]
    vectors1 = hook(vectors1, (flow0,))

    grad_pointwise = jnp.stack(
        [flow.total for flow in (flow0, flow1, flow2, flow3, flow4)]
    )
    grad_pointwise = narrow(grad_pointwise[:, :block], per_chan, block)
    kernel_part = jnp.stack([flow7.total, flow6.total])[:, :, :gw_part, :block]
    parts = [kernel_part] + [wire.swap(kernel_part, (0, d)) for d in range(1, chan)]
    bit = 1
    while bit < chan:
        high = (wire.col & bit) != 0
        parts = [jnp.where(high, parts[i ^ bit], parts[i]) for i in range(chan)]
        bit *= 2
    grad_grouped = jnp.concatenate(parts, axis=2)

    vectors = jnp.stack([vectors1, vectors2])
    pooled_all, gate_all = vectors[:, :, :block], vectors[:, :, lanes : lanes + block]
    q_all = narrow(vectors[:, :, 2 * lanes : 2 * lanes + se_full], chan, se_block)
    pre_all = narrow(vectors[:, :, 2 * lanes + se_full :], chan, se_block)
    grad_squeeze = jnp.einsum("lnk,lns->lks", pooled_all, pre_all, precision=highest)
    grad_excite = jnp.einsum("lns,lnk->lsk", q_all, gate_all, precision=highest)
    backs = [back0, back1, back2, back3, back4, back5, back6]
    grad_norm = jnp.stack([jnp.stack([b[0] for b in backs]), jnp.stack([b[1] for b in backs])])
    grad_norm = lax.dynamic_slice_in_dim(grad_norm, wire.row * lanes, lanes, 2)[:, :, :block]

    def squares(tensor, weighting):
        return weighting * jnp.sum(tensor * tensor, axis=tuple(range(1, tensor.ndim)))

    leader = (wire.col == 0).astype(f32)
    weight_list = (pointwise_w, grouped_w, squeeze_w, excite_w)
    grad_list = (grad_pointwise, grad_grouped, grad_squeeze, grad_excite)
    scales = (1.0, leader, leader, leader)
    terms = [squares(t, s) for t, s in zip(weight_list + grad_list, scales + scales)]
    terms = jnp.concatenate(terms)
    terms = wire.sum_planes(terms + wire.core(terms))
    layer_norms = jnp.sqrt(terms).reshape(2, 11)
    weight_norms, grad_norms = layer_norms[0], layer_norms[1]
    ratio = trust_coef * weight_norms / (grad_norms + weight_decay * weight_norms)

    def lars_step(weight, moment, gradient, ratios):
        scaled_rate = ratios.reshape((-1,) + (1,) * (weight.ndim - 1))
        moment_new = momentum_rate * moment + learn_rate * scaled_rate * (
            gradient + weight_decay * weight
        )
        return (moment_new, weight - moment_new)

    moment_pointwise, new_pointwise = lars_step(
        pointwise_w, pointwise_m, grad_pointwise, ratio[0:5]
    )
    moment_grouped, new_grouped = lars_step(grouped_w, grouped_m, grad_grouped, ratio[5:7])
    moment_squeeze, new_squeeze = lars_step(squeeze_w, squeeze_m, grad_squeeze, ratio[7:9])
    moment_excite, new_excite = lars_step(excite_w, excite_m, grad_excite, ratio[9:11])
    moment_norm = momentum_rate * norm_m + norm_rate * grad_norm
    new_norm = norm_params - moment_norm
    return (
        activations,
        input_grad,
        layer_norms,
        grad_pointwise,
        grad_grouped,
        grad_squeeze,
        grad_excite,
        grad_norm,
        moment_pointwise,
        moment_grouped,
        moment_squeeze,
        moment_excite,
        moment_norm,
        new_pointwise,
        new_grouped,
        new_squeeze,
        new_excite,
        new_norm,
    )


def solution(mesh):
    image = P(("rows", "chan"), None, None, None)
    point = P(None, "rows", "chan")
    grouped = P(None, None, None, "rows")
    squeeze = P(None, "rows", None)
    excite = P(None, None, "rows")
    weights = (point, grouped, squeeze, excite, excite)
    return jax.shard_map(
        per_device,
        mesh=mesh,
        in_specs=(image, P(), image) + weights + weights,
        out_specs=(image, image, P()) + weights + weights + weights,
        check_vma=False,
    )
```
